1024 devices in a mesh: replica: 64 (over y, z_hi, x), fsdp: 16 (over z_lo, core).
Axes of the slice: x: 4, y: 4, z: 32 (z_hi: 4, z_lo: 8; z = z_hi * 8 + z_lo), core: 2. Of those that a mesh axis runs over, the one named last changes fastest.
Arguments:
- tokens: bfloat16 [131072, 8192], P(('replica', 'fsdp')), may hold values from -24 to 24
- cotangent: bfloat16 [131072, 512], P(('replica', 'fsdp')), may hold values from -0.125 to 0.125
- inner_weights: bfloat16 [64, 8192, 512], P('replica', 'fsdp'), may hold values from -16 to 16
- global_weights: bfloat16 [8192, 512], P('fsdp'), may hold values from -6 to 6
- momentum: float32 [8192, 512], P(('fsdp', 'replica')), may hold values from -4 to 4
- exponents: int32 [64, 256, 4], P('replica', 'fsdp'), may hold values from -1 to 2
Outputs:
- blended: bfloat16 [64, 8192, 512], P('replica', 'fsdp')
- global_next: bfloat16 [8192, 512], P('fsdp')
- momentum_next: float32 [8192, 512], P(('fsdp', 'replica'))
The draws below stay inside these ranges and needn't reach their ends.
All inputs are finite; a program needn't handle non-finite values.
Results may differ from the reference program's by a relative error of at most 0.011.
Values may be sent and summed in bfloat16 or wider, within the bound.
A program may use at most 64 MiB of HBM per device.

```python
import jax
import jax.numpy as jnp
from jax import lax

D = 8192
TOK_DEV = 128
SROWS = 32
SCOLS = 128
KVW = 512
REPLICAS = 64
TOKENS = 131072
N_REPLICA = 64
N_FSDP = 16


def touch_ends(drawn, own_key, least, high):
    place = [jax.random.randint(jax.random.fold_in(own_key, axis), (), 0, length) for axis, length in enumerate(drawn.shape)]
    widest = drawn.shape.index(max(drawn.shape))
    neighbour = place[:widest] + [(place[widest] + 1) % drawn.shape[widest]] + place[widest + 1:]
    return drawn.at[tuple(place)].set(least).at[tuple(neighbour)].set(high)


def with_spikes(entries, key, source, target, shards_of, factor):
    owner, partner = [(jnp.arange(entries.shape[axis_at]) // (entries.shape[axis_at] // shards_of)).reshape([-1 if axis == axis_at else 1 for axis in range(entries.ndim)]) for axis_at in (source, target)]
    chosen = jax.random.permutation(key, shards_of)[partner]
    strong = (owner == chosen) | (owner == (partner + shards_of // 2) % shards_of)
    return jnp.where(strong, factor * entries, entries)


def shard_levels(own_key, dims, pieces, low, high):
    def one(position, parts):
        draws = jax.random.uniform(jax.random.fold_in(jax.random.fold_in(own_key, 6), position), (parts,), jnp.float32, low / len(pieces), high / len(pieces))
        return jnp.repeat(jnp.exp(draws), dims[position] // parts).reshape((-1,) + (1,) * (len(dims) - position - 1))

    level = one(*pieces[0])
    for cut in pieces[1:]:
        level = level * one(*cut)
    return level


def normal_values(stream_key, dims, spread, reach, cuts=(), kind=jnp.bfloat16):
    loudness = shard_levels(stream_key, dims, cuts, -0.22, 0.18) if cuts else 1.0
    values = jax.random.normal(stream_key, dims, jnp.float32) * spread * loudness
    return jnp.minimum(jnp.maximum(values, -reach), reach).astype(kind)


def noise_with(rng, dims, spread, limit, split, heavy, held_as=jnp.bfloat16):
    entries = spread * jax.random.normal(rng, dims, jnp.float32)
    if split:
        entries = entries * shard_levels(rng, dims, split, -0.22, 0.18)
    return jnp.clip(with_spikes(entries, jax.random.fold_in(rng, 3), *heavy), -limit, limit).astype(held_as)


def setup_inputs(seed: int = 0) -> dict:
    key_list = jax.random.split(jax.random.key(seed), 7)
    tokens = noise_with(key_list[0], (TOKENS, D), 1.0, 24.0, ((0, 1024),), (0, 1, 1024, 6.0))
    cotangent = normal_values(key_list[1], (TOKENS, KVW), (TOK_DEV * N_FSDP) ** -0.5, 0.125, ((0, 1024),))
    inner_weights = noise_with(key_list[2], (REPLICAS, D, KVW), 1.0, 16.0, ((0, 64), (1, 16)), (0, 1, 64, 4.0))
    global_weights = normal_values(key_list[3], (D, KVW), 1.0, 6.0, ((0, 16),))
    momentum = normal_values(key_list[4], (D, KVW), 0.5, 4.0, ((0, 1024),), jnp.float32)
    exponents = touch_ends(jax.random.randint(key_list[5], (REPLICAS, D // SROWS, KVW // SCOLS), -1, 3), jax.random.fold_in(key_list[5], 1), -1, 2).astype(jnp.int32)
    return dict(tokens=tokens, cotangent=cotangent, inner_weights=inner_weights, global_weights=global_weights, momentum=momentum, exponents=exponents)


clip_level = 2.0
inner_rate = 0.5
outer_rate = 0.7
outer_momentum = 0.9
mixing = 0.5


def expand_scales(exponent_block):
    powers = jnp.exp2(exponent_block.astype(jnp.float32))
    return jnp.repeat(jnp.repeat(powers, SROWS, axis=0), SCOLS, axis=1)


def decode_one(global_weights, inner_one, exponent_block):
    block_scale = expand_scales(exponent_block)
    pseudo_grad = global_weights.astype(jnp.float32) - inner_one.astype(jnp.float32)
    encoded = jnp.clip(pseudo_grad / block_scale, -clip_level, clip_level).astype(jnp.bfloat16)
    return encoded.astype(jnp.float32) * block_scale


def reference(tokens, cotangent, inner_weights, global_weights, momentum, exponents):
    def add_one(summed, pair):
        inner_one, exponent_block = pair
        return summed + decode_one(global_weights, inner_one, exponent_block), None

    summed, _ = lax.scan(add_one, jnp.zeros((D, KVW), jnp.float32), (inner_weights, exponents))
    average = summed / N_REPLICA
    momentum_next = outer_momentum * momentum + average
    global_next = (global_weights.astype(jnp.float32) - outer_rate * (outer_momentum * momentum_next + average)).astype(jnp.bfloat16)
    grouped_tokens = tokens.reshape(N_REPLICA, TOK_DEV * N_FSDP, D)
    grouped_cot = cotangent.reshape(N_REPLICA, TOK_DEV * N_FSDP, KVW)

    def blend_one(triple):
        token_rows, cot_rows, inner_one = triple
        gradient = jnp.dot(token_rows.T, cot_rows, preferred_element_type=jnp.float32)
        stepped = inner_one.astype(jnp.float32) - inner_rate * gradient
        return (mixing * stepped + (1.0 - mixing) * global_next.astype(jnp.float32)).astype(jnp.bfloat16)

    blended = lax.map(blend_one, (grouped_tokens, grouped_cot, inner_weights))
    return (blended, global_next, momentum_next)
```

```python
import functools

import jax
import jax.numpy as jnp
from jax import lax
from jax.experimental import pallas as pl
from jax.experimental.pallas import tpu as pltpu
from jax.sharding import PartitionSpec as P

MESH = pl.DeviceIdType.MESH
F32 = jnp.float32
BF16 = jnp.bfloat16

CHIPS = 8
TOK = 128
BLK = 512
QR = 128
HC = 256
NQ = BLK // QR
NH = BLK // HC
NC = NQ * NH
LAG = 4
STAGES = (8, 15, 21, 27, 32, 38)


def kernel(
    dims,
    replicas,
    tok,
    cot,
    inner,
    glob,
    mom,
    expo,
    blended,
    gnext,
    mnext,
    t_own,
    t_ext,
    c_own,
    c_ext,
    up_buf,
    dn_buf,
    acc,
    inner_v,
    glob_v,
    mom_v,
    out_v,
    gn_v,
    mn_v,
    dec,
    got1,
    part2,
    got2,
    part3,
    got3,
    gath,
    in_sem,
    tin_sem,
    sib_send,
    sib_recv,
    cx_send,
    cx_recv,
    tx_send,
    tx_recv,
    up_send,
    up_recv,
    dn_send,
    dn_recv,
    st_send,
    st_recv,
    out_sem,
):
    ny, nz, nx = dims
    r = lax.axis_index("replica")
    f = lax.axis_index("fsdp")
    i = f // 2
    c = lax.rem(f, 2)
    x = lax.rem(r, nx)
    z = lax.rem(r // nx, nz)
    y = r // (nx * nz)
    sib = (r, f + 1 - 2 * c)
    low_end, high_end = i == 0, i == CHIPS - 1
    is_end = low_end | high_end
    is_next = (i == 1) | (i == CHIPS - 2)
    paired = is_end | is_next
    mate_i = i + 1 - 2 * lax.rem(i, 2)
    mate = (r, 2 * mate_i + c)
    cross = (r, 2 * mate_i + 1 - c)
    above = (r, jnp.minimum(f + 2, 2 * CHIPS - 1))
    below = (r, jnp.maximum(f - 2, 0))

    def at(yy, zz, xx):
        return ((yy * nz + zz) * nx + xx, f)

    x_peers = [at(y, z, lax.rem(x + k, nx)) for k in range(1, nx)]
    y_peers = [at(lax.rem(y + k, ny), z, x) for k in range(1, ny)]
    z_peers = [at(y, lax.rem(z + k, nz), x) for k in range(1, nz)]

    def t_copy(d):
        return pltpu.make_async_copy(
            tok.at[:, pl.ds(pl.multiple_of((2 * d + c) * BLK, BLK), BLK)],
            t_own.at[0:TOK, pl.ds(pl.multiple_of(d * BLK, BLK), BLK)],
            tin_sem.at[d],
        )

    c_copy = pltpu.make_async_copy(cot, c_own.at[0:TOK], in_sem.at[0])
    i_copy = pltpu.make_async_copy(inner, inner_v, in_sem.at[1])
    g_copy = pltpu.make_async_copy(glob, glob_v, in_sem.at[2])
    m_copy = pltpu.make_async_copy(mom, mom_v, in_sem.at[3])
    i_copy.start()
    g_copy.start()
    c_copy.start()
    m_copy.start()

    @pl.loop(0, CHIPS)
    def _(d):
        t_copy(d).start()

    barrier = pltpu.get_barrier_semaphore()
    for peer in [sib] + x_peers + y_peers + z_peers:
        pl.semaphore_signal(barrier, 1, device_id=peer, device_id_type=MESH)

    @pl.when(i < CHIPS - 1)
    def _():
        pl.semaphore_signal(barrier, 1, device_id=above, device_id_type=MESH)

    @pl.when(i > 0)
    def _():
        pl.semaphore_signal(barrier, 1, device_id=below, device_id_type=MESH)

    @pl.when(paired)
    def _():
        pl.semaphore_signal(barrier, 1, device_id=cross, device_id_type=MESH)

    others = 1 + (nx - 1) + (ny - 1) + (nz - 1)
    pl.semaphore_wait(
        barrier,
        others + jnp.where(is_end, 1, 2) + jnp.where(paired, 1, 0),
    )

    def cx_copy():
        return pltpu.make_async_remote_copy(
            cot, c_ext.at[0:TOK], cx_send.at[0], cx_recv.at[0], device_id=mate, device_id_type=MESH
        )

    def cx_forward():
        return pltpu.make_async_remote_copy(
            c_ext.at[0:TOK],
            c_ext.at[TOK : 2 * TOK],
            cx_send.at[1],
            cx_recv.at[1],
            device_id=sib,
            device_id_type=MESH,
        )

    def tx_copy(k, q, other):
        d = jnp.where((i == 0) | (i == 1), CHIPS - 1 - k, k)
        src_c = (1 - c) if other else c
        return pltpu.make_async_remote_copy(
            tok.at[:, pl.ds(pl.multiple_of((2 * d + src_c) * BLK + q * QR, QR), QR)],
            t_ext.at[
                (TOK if other else 0) : (2 * TOK if other else TOK),
                pl.ds(pl.multiple_of(d * BLK + q * QR, QR), QR),
            ],
            tx_send.at[1 if other else 0],
            tx_recv.at[k * NQ + q, 1 if other else 0],
            device_id=cross if other else mate,
            device_id_type=MESH,
        )

    @pl.when(is_end)
    def _():
        cx_copy().start()

        @pl.loop(0, (CHIPS - 1) * NQ)
        def _(n):
            tx_copy(n // NQ, lax.rem(n, NQ), False).start()
            tx_copy(n // NQ, lax.rem(n, NQ), True).start()

    sc_copy = pltpu.make_async_remote_copy(
        cot,
        c_own.at[TOK : 2 * TOK],
        sib_send.at[CHIPS],
        sib_recv.at[CHIPS],
        device_id=sib,
        device_id_type=MESH,
    )

    def st_copy(d):
        return pltpu.make_async_remote_copy(
            tok.at[:, pl.ds(pl.multiple_of((2 * d + 1 - c) * BLK, BLK), BLK)],
            t_own.at[TOK : 2 * TOK, pl.ds(pl.multiple_of(d * BLK, BLK), BLK)],
            sib_send.at[d],
            sib_recv.at[d],
            device_id=sib,
            device_id_type=MESH,
        )

    sc_copy.start()

    @pl.loop(0, CHIPS)
    def _(d):
        st_copy(d).start()

    i_copy.wait()
    g_copy.wait()

    @pl.loop(0, BLK // 16)
    def _(t):
        rows = pl.ds(pl.multiple_of(t * 16, 16), 16)
        diff = glob_v[rows, :].astype(F32) - inner_v[rows, :].astype(F32)
        parts = []
        for b in range(4):
            e = expo[t // 2, b]
            lim = jnp.where(e < 0, 1.0, jnp.where(e == 0, 2.0, jnp.where(e == 1, 4.0, 8.0)))
            parts.append(jnp.clip(diff[:, b * 128 : (b + 1) * 128], -lim, lim))
        for half in range(2):
            rr = 2 * t + half
            packed = jnp.concatenate([p[8 * half : 8 * half + 8] for p in parts], axis=0)
            rx = lax.rem(rr, nx)
            rz = lax.rem(rr // nx, nz)
            ry = rr // (nx * nz)
            dec[rx, ry * nz + rz] = packed.astype(BF16)

    def stage_copy(stage, k, src, dst, peer):
        return pltpu.make_async_remote_copy(
            src, dst, st_send.at[stage, k], st_recv.at[stage, k], device_id=peer, device_id_type=MESH
        )

    def x_sum(k):
        return stage_copy(0, k, dec.at[lax.rem(x + k + 1, nx)], got1.at[k], x_peers[k])

    def y_sum(k):
        return stage_copy(1, k, part2.at[lax.rem(y + k + 1, ny)], got2.at[k], y_peers[k])

    def z_sum(k):
        return stage_copy(2, k, part3.at[lax.rem(z + k + 1, nz)], got3.at[k], z_peers[k])

    def z_gather(k, zz):
        ref = gath.at[x, y, zz]
        return stage_copy(3, k, ref, ref, z_peers[k])

    def y_gather(k, yy):
        ref = gath.at[x, yy]
        return stage_copy(4, k, ref, ref, y_peers[k])

    def x_gather(k, xx):
        ref = gath.at[xx]
        return stage_copy(5, k, ref, ref, x_peers[k])

    for k in range(nx - 1):
        x_sum(k).start()

    @pl.when(is_next)
    def _():
        cx_copy().wait_recv()
        cx_forward().start()

    c_copy.wait()

    @pl.loop(0, CHIPS)
    def _(d):
        t_copy(d).wait()
        st_copy(d).wait_recv()

    sc_copy.wait_recv()

    @pl.when(is_next)
    def _():
        cx_forward().wait_recv()

    def share(d, q, h, extra, k):
        cols = pl.ds(pl.multiple_of(d * BLK + q * QR, QR), QR)
        kv = pl.ds(pl.multiple_of(h * HC, HC), HC)
        contract = (((0,), (0,)), ((), ()))
        acc[...] = lax.dot_general(
            t_own[:, cols], c_own[:, kv], contract, preferred_element_type=F32
        )

        @pl.when(extra)
        def _():
            @pl.when(h == 0)
            def _():
                tx_copy(k, q, False).wait_recv()
                tx_copy(k, q, True).wait_recv()

            acc[...] += lax.dot_general(
                t_ext[:, cols], c_ext[:, kv], contract, preferred_element_type=F32
            )

    def up_copy(n):
        return pltpu.make_async_remote_copy(
            up_buf.at[n], up_buf.at[n], up_send.at[n // NC], up_recv.at[n], device_id=above, device_id_type=MESH
        )

    def dn_copy(n):
        return pltpu.make_async_remote_copy(
            dn_buf.at[n], dn_buf.at[n], dn_send.at[n // NC], dn_recv.at[n], device_id=below, device_id_type=MESH
        )

    ticks = (CHIPS - 2) * NC

    @pl.loop(0, ticks)
    def _(t):
        su = t - (i - 1) * LAG
        ku = su // NC

        @pl.when((i >= 1) & (su >= 0) & (su < (CHIPS - 1 - i) * NC))
        def _():
            d = CHIPS - 1 - ku
            p = lax.rem(su, NC)
            n = d * NC + p
            share(d, p // NH, lax.rem(p, NH), i == 1, ku)

            @pl.when(i > 1)
            def _():
                up_copy(n).wait_recv()
                up_buf[n] = (acc[...] + up_buf[n].astype(F32)).astype(BF16)

            @pl.when(i == 1)
            def _():
                up_buf[n] = acc[...].astype(BF16)

            up_copy(n).start()

        sd = t - (CHIPS - 2 - i) * LAG
        kd = sd // NC

        @pl.when((i <= CHIPS - 2) & (sd >= 0) & (sd < i * NC))
        def _():
            p = lax.rem(sd, NC)
            n = kd * NC + p
            share(kd, p // NH, lax.rem(p, NH), i == CHIPS - 2, kd)

            @pl.when(i < CHIPS - 2)
            def _():
                dn_copy(n).wait_recv()
                dn_buf[n] = (acc[...] + dn_buf[n].astype(F32)).astype(BF16)

            @pl.when(i == CHIPS - 2)
            def _():
                dn_buf[n] = acc[...].astype(BF16)

            dn_copy(n).start()

        @pl.when(t == STAGES[0])
        def _():
            for k in range(nx - 1):
                x_sum(k).wait_recv()

            @pl.loop(0, ny * nz)
            def _(g):
                total = dec[x, g].astype(F32)
                for k in range(nx - 1):
                    total += got1[k, g].astype(F32)
                part2[g // nz, lax.rem(g, nz)] = total.astype(BF16)

            for k in range(ny - 1):
                y_sum(k).start()

        @pl.when(t == STAGES[1])
        def _():
            for k in range(ny - 1):
                y_sum(k).wait_recv()
            for g in range(nz):
                total = part2[y, g].astype(F32)
                for k in range(ny - 1):
                    total += got2[k, g].astype(F32)
                part3[g] = total.astype(BF16)
            for k in range(nz - 1):
                z_sum(k).start()

        @pl.when(t == STAGES[2])
        def _():
            for k in range(nz - 1):
                z_sum(k).wait_recv()
            total = part3[z].astype(F32)
            for k in range(nz - 1):
                total += got3[k].astype(F32)
            average = total / replicas
            m_copy.wait()
            mom_now = mom_v[...]
            mom_p = jnp.concatenate([mom_now[:, b * 128 : (b + 1) * 128] for b in range(4)], axis=0)
            mom_next = 0.9 * mom_p + average
            own = glob_v[pl.ds(pl.multiple_of(r // 2 * 16, 16), 16), :].astype(F32)
            own = jnp.where(lax.rem(r, 2) == 0, own[0:8], own[8:16])
            own_p = jnp.concatenate([own[:, b * 128 : (b + 1) * 128] for b in range(4)], axis=0)
            gath[x, y, z] = (own_p - 0.7 * (0.9 * mom_next + average)).astype(BF16)
            for k in range(nz - 1):
                z_gather(k, z).start()
            for b in range(4):
                mn_v[:, b * 128 : (b + 1) * 128] = mom_next[8 * b : 8 * b + 8]
            pltpu.make_async_copy(mn_v, mnext, out_sem.at[0]).start()

        @pl.when(t == STAGES[3])
        def _():
            for k in range(nz - 1):
                z_gather(k, lax.rem(z + nz - k - 1, nz)).wait_recv()
            for k in range(ny - 1):
                y_gather(k, y).start()

        @pl.when(t == STAGES[4])
        def _():
            for k in range(ny - 1):
                y_gather(k, lax.rem(y + ny - k - 1, ny)).wait_recv()
            for k in range(nx - 1):
                x_gather(k, x).start()

        @pl.when(t == STAGES[5])
        def _():
            for k in range(nx - 1):
                x_gather(k, lax.rem(x + nx - k - 1, nx)).wait_recv()

            @pl.loop(0, BLK // 16)
            def _(n):
                halves = []
                for half in range(2):
                    rr = 2 * n + half
                    piece = gath[lax.rem(rr, nx), rr // (nx * nz), lax.rem(rr // nx, nz)].astype(F32)
                    halves.append(
                        jnp.concatenate([piece[8 * b : 8 * b + 8] for b in range(4)], axis=1)
                    )
                gn_v[pl.ds(pl.multiple_of(n * 16, 16), 16), :] = jnp.concatenate(
                    halves, axis=0
                ).astype(BF16)

            pltpu.make_async_copy(gn_v, gnext, out_sem.at[1]).start()

    def out_copy(q):
        rows = pl.ds(pl.multiple_of(q * QR, QR), QR)
        return pltpu.make_async_copy(out_v.at[rows], blended.at[rows], out_sem.at[2 + q])

    @pl.loop(0, NC)
    def _(p):
        q, h = p // NH, lax.rem(p, NH)
        n = i * NC + p
        share(i, q, h, is_next, CHIPS - 2)

        @pl.when(i <= CHIPS - 3)
        def _():
            dn_copy(n).wait_recv()
            acc[...] += dn_buf[n].astype(F32)

        @pl.when(i >= 2)
        def _():
            up_copy(n).wait_recv()
            acc[...] += up_buf[n].astype(F32)

        rows = pl.ds(pl.multiple_of(q * QR, QR), QR)
        kv = pl.ds(pl.multiple_of(h * HC, HC), HC)
        stepped = inner_v[rows, kv].astype(F32) - 0.5 * acc[...]
        out_v[rows, kv] = (0.5 * stepped + 0.5 * gn_v[rows, kv].astype(F32)).astype(BF16)

        @pl.when(h == NH - 1)
        def _():
            out_copy(q).start()

    sc_copy.wait_send()

    @pl.loop(0, CHIPS)
    def _(d):
        st_copy(d).wait_send()

    @pl.when(is_next)
    def _():
        cx_forward().wait_send()

    @pl.when(is_end)
    def _():
        cx_copy().wait_send()
        for other in range(2):
            whole = t_ext.at[0:TOK, 0 : (CHIPS - 1) * BLK]
            pltpu.make_async_copy(whole, whole, tx_send.at[other]).wait()

    def wait_block(buf, sem, d):
        whole = buf.at[pl.ds(d * NC, NC)]
        pltpu.make_async_copy(whole, whole, sem.at[d]).wait()

    @pl.loop(0, CHIPS)
    def _(d):
        @pl.when((i >= 1) & (d > i))
        def _():
            wait_block(up_buf, up_send, d)

        @pl.when((i <= CHIPS - 2) & (d < i))
        def _():
            wait_block(dn_buf, dn_send, d)

    for k in range(nx - 1):
        x_sum(k).wait_send()
        x_gather(k, x).wait_send()
    for k in range(ny - 1):
        y_sum(k).wait_send()
        y_gather(k, y).wait_send()
    for k in range(nz - 1):
        z_sum(k).wait_send()
        z_gather(k, z).wait_send()
    pltpu.make_async_copy(mn_v, mnext, out_sem.at[0]).wait()
    pltpu.make_async_copy(gn_v, gnext, out_sem.at[1]).wait()
    for q in range(NQ):
        out_copy(q).wait()


def body(dims, tokens, cotangent, inner_weights, global_weights, momentum, exponents):
    ny, nz, nx = dims
    replicas = ny * nz * nx
    anywhere = pl.BlockSpec(memory_space=pl.ANY)
    sem = pltpu.SemaphoreType.DMA
    blended, gnext, mnext = pl.pallas_call(
        functools.partial(kernel, dims, replicas),
        out_shape=(
            jax.ShapeDtypeStruct((BLK, BLK), BF16),
            jax.ShapeDtypeStruct((BLK, BLK), BF16),
            jax.ShapeDtypeStruct((8, BLK), F32),
        ),
        in_specs=[anywhere] * 5 + [pl.BlockSpec(memory_space=pltpu.SMEM)],
        out_specs=(anywhere,) * 3,
        scratch_shapes=[
            pltpu.VMEM((2 * TOK, CHIPS * BLK), BF16),
            pltpu.VMEM((2 * TOK, CHIPS * BLK), BF16),
            pltpu.VMEM((2 * TOK, BLK), BF16),
            pltpu.VMEM((2 * TOK, BLK), BF16),
            pltpu.VMEM((CHIPS * NC, QR, HC), BF16),
            pltpu.VMEM((CHIPS * NC, QR, HC), BF16),
            pltpu.VMEM((QR, HC), F32),
            pltpu.VMEM((BLK, BLK), BF16),
            pltpu.VMEM((BLK, BLK), BF16),
            pltpu.VMEM((8, BLK), F32),
            pltpu.VMEM((BLK, BLK), BF16),
            pltpu.VMEM((BLK, BLK), BF16),
            pltpu.VMEM((8, BLK), F32),
            pltpu.VMEM((nx, 64 // nx, 32, 128), BF16),
            pltpu.VMEM((3, ny * nz, 32, 128), BF16),
            pltpu.VMEM((ny, nz, 32, 128), BF16),
            pltpu.VMEM((3, nz, 32, 128), BF16),
            pltpu.VMEM((nz, 32, 128), BF16),
            pltpu.VMEM((3, 32, 128), BF16),
            pltpu.VMEM((nx, 64 // (nx * nz), nz, 32, 128), BF16),
            sem((4,)),
            sem((CHIPS,)),
            sem((CHIPS + 1,)),
            sem((CHIPS + 1,)),
            sem((2,)),
            sem((2,)),
            sem((2,)),
            sem(((CHIPS - 1) * NQ, 2)),
            sem((CHIPS,)),
            sem((CHIPS * NC,)),
            sem((CHIPS,)),
            sem((CHIPS * NC,)),
            sem((6, 3)),
            sem((6, 3)),
            sem((2 + NQ,)),
        ],
        compiler_params=pltpu.CompilerParams(
            collective_id=0, has_side_effects=True, vmem_limit_bytes=48 << 20
        ),
    )(tokens, cotangent, inner_weights[0], global_weights, momentum, exponents[0])
    return blended[None], gnext, mnext


def solution(mesh):
    return jax.shard_map(
        functools.partial(body, (4, 4, 4)),
        mesh=mesh,
        in_specs=(
            P(("replica", "fsdp"), None),
            P(("replica", "fsdp"), None),
            P("replica", "fsdp", None),
            P("fsdp", None),
            P(("fsdp", "replica"), None),
            P("replica", "fsdp", None),
        ),
        out_specs=(P("replica", "fsdp", None), P("fsdp", None), P(("fsdp", "replica"), None)),
        check_vma=False,
    )
```

```python
import functools

import jax
import jax.numpy as jnp
from jax import lax
from jax.experimental import pallas as pl
from jax.experimental.pallas import tpu as pltpu
from jax.sharding import PartitionSpec as P

MESH = pl.DeviceIdType.MESH
F32 = jnp.float32
BF16 = jnp.bfloat16

CHIPS = 8
TOK = 128
BLK = 512
QR = 128
HC = 512
NQ = BLK // QR
NH = BLK // HC
NC = NQ * NH
LAG = 3
DECODE = 1
STAGES = (
    (4, 4, 4, 4),
    (7, 7, 6, 6),
    (12, 10, 9, 10),
    (15, 13, 12, 12),
    (17, 15, 14, 15),
    (19, 18, 17, 17),
    (21, 19, 18, 19),
    (23, 22, 21, 22),
)


def kernel(
    dims,
    replicas,
    tok,
    cot,
    inner,
    glob,
    mom,
    expo,
    out_v,
    gn_v,
    mn_v,
    t_own,
    t_ext,
    c_own,
    c_ext,
    up_buf,
    dn_buf,
    acc,
    inner_v,
    glob_v,
    mom_v,
    dec,
    got1,
    part2,
    got2,
    part3,
    far3,
    got3,
    gath,
    in_sem,
    tin_sem,
    sib_send,
    sib_recv,
    cx_send,
    cx_recv,
    tx_send,
    tx_recv,
    up_send,
    up_recv,
    dn_send,
    dn_recv,
    st_send,
    st_recv,
    tok_go,
):
    ny, nz, nx = dims
    r = lax.axis_index("replica")
    f = lax.axis_index("fsdp")
    i = f // 2
    c = lax.rem(f, 2)
    x = lax.rem(r, nx)
    z = lax.rem(r // nx, nz)
    y = r // (nx * nz)
    sib = (r, f + 1 - 2 * c)
    low_end, high_end = i == 0, i == CHIPS - 1
    is_end = low_end | high_end
    is_next = (i == 1) | (i == CHIPS - 2)
    paired = is_end | is_next
    mate_i = i + 1 - 2 * lax.rem(i, 2)
    mate = (r, 2 * mate_i + c)
    cross = (r, 2 * mate_i + 1 - c)
    above = (r, jnp.minimum(f + 2, 2 * CHIPS - 1))
    below = (r, jnp.maximum(f - 2, 0))

    def at(yy, zz, xx):
        return ((yy * nz + zz) * nx + xx, f)

    x_peers = [at(y, z, lax.rem(x + k, nx)) for k in range(1, nx)]
    y_peers = [at(lax.rem(y + k, ny), z, x) for k in range(1, ny)]

    def t_copy(d):
        return pltpu.make_async_copy(
            tok.at[:, pl.ds(pl.multiple_of((2 * d + c) * BLK, BLK), BLK)],
            t_own.at[0:TOK, pl.ds(pl.multiple_of(d * BLK, BLK), BLK)],
            tin_sem.at[d],
        )

    c_copy = pltpu.make_async_copy(cot, c_own.at[0:TOK], in_sem.at[0])
    i_copy = pltpu.make_async_copy(inner, inner_v, in_sem.at[1])
    g_copy = pltpu.make_async_copy(glob, glob_v, in_sem.at[2])
    m_copy = pltpu.make_async_copy(mom, mom_v, in_sem.at[3])
    i_copy.start()
    g_copy.start()
    c_copy.start()
    m_copy.start()

    @pl.loop(0, CHIPS)
    def _(d):
        t_copy(d).start()

    root = min(2, nz - 1)
    leader_i = jnp.where((z == root) & (nz > 1), CHIPS // 2 - 1, CHIPS - 1)
    leader = i == leader_i
    line = [(r, lax.rem(f + 2 * k, 2 * CHIPS)) for k in range(1, CHIPS)]

    def at_z(zz):
        return at(y, zz, x)

    def signal(semaphore, peer):
        pl.semaphore_signal(semaphore, 1, device_id=peer, device_id_type=MESH)

    barrier = pltpu.get_barrier_semaphore()
    for peer in [sib] + x_peers + y_peers:
        signal(barrier, peer)

    @pl.when(i < CHIPS - 1)
    def _():
        signal(barrier, above)

    @pl.when(i > 0)
    def _():
        signal(barrier, below)

    @pl.when(paired)
    def _():
        signal(barrier, cross)

    @pl.when((i < leader_i - 1) | (i > leader_i + 1))
    def _():
        signal(barrier, (r, 2 * leader_i + c))

    near = jnp.where(leader, CHIPS - 1 + jnp.where(z == root, nz - 1, 0), jnp.where(is_end, 1, 2))
    pl.semaphore_wait(barrier, 1 + (nx - 1) + (ny - 1) + near + jnp.where(paired, 1, 0))

    if nz > 1:

        @pl.when(leader & (z != root))
        def _():
            signal(barrier, (at_z(root)[0], 2 * (CHIPS // 2 - 1) + c))

    def all_groups():
        @pl.when(z == root)
        def _():
            for k in range(1, nz):
                signal(tok_go, (at_z(lax.rem(z + k, nz))[0], 2 * (CHIPS - 1) + c))

        @pl.when(z != root)
        def _():
            pl.semaphore_wait(tok_go, 1)

        for peer in line:
            signal(tok_go, peer)

    def cx_copy(h):
        cols = slice(h * 256, h * 256 + 256)
        return pltpu.make_async_remote_copy(
            cot.at[:, cols],
            c_ext.at[0:TOK, cols],
            cx_send.at[h],
            cx_recv.at[h],
            device_id=mate,
            device_id_type=MESH,
        )

    def cx_forward(h):
        cols = slice(h * 256, h * 256 + 256)
        return pltpu.make_async_remote_copy(
            c_ext.at[0:TOK, cols],
            c_ext.at[TOK : 2 * TOK, cols],
            cx_send.at[2 + h],
            cx_recv.at[2 + h],
            device_id=sib,
            device_id_type=MESH,
        )

    def tx_copy(k, q, width, n, other):
        d = jnp.where((i == 0) | (i == 1), CHIPS - 1 - k, k)
        src_c = (1 - c) if other else c
        return pltpu.make_async_remote_copy(
            tok.at[:, pl.ds(pl.multiple_of((2 * d + src_c) * BLK + q * QR, QR), width)],
            t_ext.at[
                (TOK if other else 0) : (2 * TOK if other else TOK),
                pl.ds(pl.multiple_of(d * BLK + q * QR, QR), width),
            ],
            tx_send.at[1 if other else 0],
            tx_recv.at[n, 1 if other else 0],
            device_id=cross if other else mate,
            device_id_type=MESH,
        )

    def tx_part(q, other):
        return tx_copy(0, q, QR, q, other)

    def tx_whole(k, other):
        return tx_copy(k, 0, BLK, NQ - 1 + k, other)

    @pl.when(is_end)
    def _():
        cx_copy(0).start()
        tx_part(0, False).start()
        tx_part(0, True).start()
        cx_copy(1).start()

        @pl.loop(1, NQ)
        def _(q):
            tx_part(q, False).start()
            tx_part(q, True).start()

        @pl.loop(1, CHIPS - 1)
        def _(k):
            tx_whole(k, False).start()
            tx_whole(k, True).start()

    sc_copy = pltpu.make_async_remote_copy(
        cot,
        c_own.at[TOK : 2 * TOK],
        sib_send.at[CHIPS],
        sib_recv.at[CHIPS],
        device_id=sib,
        device_id_type=MESH,
    )

    def st_copy(d):
        return pltpu.make_async_remote_copy(
            tok.at[:, pl.ds(pl.multiple_of((2 * d + 1 - c) * BLK, BLK), BLK)],
            t_own.at[TOK : 2 * TOK, pl.ds(pl.multiple_of(d * BLK, BLK), BLK)],
            sib_send.at[d],
            sib_recv.at[d],
            device_id=sib,
            device_id_type=MESH,
        )

    sc_copy.start()

    @pl.loop(0, CHIPS)
    def _(d):
        st_copy(d).start()

    def stage_copy(stage, k, src, dst, peer):
        return pltpu.make_async_remote_copy(
            src, dst, st_send.at[stage, k], st_recv.at[stage, k], device_id=peer, device_id_type=MESH
        )

    def x_sum(k):
        return stage_copy(0, k, dec.at[lax.rem(x + k + 1, nx)], got1.at[k], x_peers[k])

    def y_sum(k):
        return stage_copy(1, k, part2.at[lax.rem(y + k + 1, ny)], got2.at[k], y_peers[k])

    z_next = [at_z(lax.rem(z + 1, nz)), at_z(lax.rem(z + nz - 1, nz))]
    half = [slice(0, 16), slice(16, 32)]

    def z_far(k):
        src = part3.at[lax.rem(z + 2, nz), half[k]]
        return stage_copy(2, k, src, far3.at[k], z_next[k])

    def z_sum(k):
        src = part3.at[lax.rem(z + (1, nz - 1)[k], nz)]
        return stage_copy(3, k, src, got3.at[k], z_next[k])

    def z_gather(k, zz):
        ref = gath.at[x, y, zz]
        return stage_copy(4, k, ref, ref, z_next[k])

    def z_pass(k, zz):
        ref = gath.at[x, y, zz, half[k]]
        return stage_copy(5, k, ref, ref, z_next[k])

    def y_gather(k, yy):
        ref = gath.at[x, yy]
        return stage_copy(6, k, ref, ref, y_peers[k])

    def x_gather(k, xx):
        ref = gath.at[xx]
        return stage_copy(7, k, ref, ref, x_peers[k])

    @pl.when(is_next)
    def _():
        for h in range(2):
            cx_copy(h).wait_recv()
            cx_forward(h).start()

    def t_wait(d):
        t_copy(d).wait()
        st_copy(d).wait_recv()

    c_copy.wait()
    sc_copy.wait_recv()
    t_wait(CHIPS - 1)
    t_wait(0)

    @pl.when(is_next)
    def _():
        for h in range(2):
            cx_forward(h).wait_recv()

    def share(d, q, h, extra, k):
        cols = pl.ds(pl.multiple_of(d * BLK + q * QR, QR), QR)
        kv = pl.ds(pl.multiple_of(h * HC, HC), HC)
        contract = (((0,), (0,)), ((), ()))
        acc[...] = lax.dot_general(
            t_own[:, cols], c_own[:, kv], contract, preferred_element_type=F32
        )

        @pl.when(extra)
        def _():
            @pl.when((h == 0) & (k == 0))
            def _():
                tx_part(q, False).wait_recv()
                tx_part(q, True).wait_recv()

            @pl.when((h == 0) & (q == 0) & (k > 0))
            def _():
                tx_whole(k, False).wait_recv()
                tx_whole(k, True).wait_recv()

            acc[...] += lax.dot_general(
                t_ext[:, cols], c_ext[:, kv], contract, preferred_element_type=F32
            )

    def up_copy(n):
        return pltpu.make_async_remote_copy(
            up_buf.at[n], up_buf.at[n], up_send.at[n // NC], up_recv.at[n], device_id=above, device_id_type=MESH
        )

    def dn_copy(n):
        return pltpu.make_async_remote_copy(
            dn_buf.at[n], dn_buf.at[n], dn_send.at[n // NC], dn_recv.at[n], device_id=below, device_id_type=MESH
        )

    def due(stage, t):
        when = STAGES[stage][0]
        for group in range(1, 4):
            when = jnp.where(z == group, STAGES[stage][group], when)
        return t == when

    ticks = (CHIPS - 2) * NC

    @pl.loop(0, ticks)
    def _(t):
        su = t - (i - 1) * LAG
        ku = su // NC

        @pl.when((i >= 1) & (su >= 0) & (su < (CHIPS - 1 - i) * NC))
        def _():
            d = CHIPS - 1 - ku
            p = lax.rem(su, NC)
            n = d * NC + p
            share(d, p // NH, lax.rem(p, NH), i == 1, ku)

            @pl.when(i > 1)
            def _():
                up_copy(n).wait_recv()
                up_buf[n] = (acc[...] + up_buf[n].astype(F32)).astype(BF16)

            @pl.when(i == 1)
            def _():
                up_buf[n] = acc[...].astype(BF16)

            up_copy(n).start()

        sd = t - (CHIPS - 2 - i) * LAG
        kd = sd // NC

        @pl.when((i <= CHIPS - 2) & (sd >= 0) & (sd < i * NC))
        def _():
            p = lax.rem(sd, NC)
            n = kd * NC + p
            share(kd, p // NH, lax.rem(p, NH), i == CHIPS - 2, kd)

            @pl.when(i < CHIPS - 2)
            def _():
                dn_copy(n).wait_recv()
                dn_buf[n] = (acc[...] + dn_buf[n].astype(F32)).astype(BF16)

            @pl.when(i == CHIPS - 2)
            def _():
                dn_buf[n] = acc[...].astype(BF16)

            dn_copy(n).start()

        @pl.when(t == DECODE)
        def _():
            @pl.loop(1, CHIPS - 1)
            def _(d):
                t_wait(d)

            i_copy.wait()
            g_copy.wait()

            @pl.loop(0, BLK // 16)
            def _(t):
                rows = pl.ds(pl.multiple_of(t * 16, 16), 16)
                diff = glob_v[rows, :].astype(F32) - inner_v[rows, :].astype(F32)
                parts = []
                for b in range(4):
                    e = expo[b, t // 2]
                    lim = jnp.where(e < 0, 1.0, jnp.where(e == 0, 2.0, jnp.where(e == 1, 4.0, 8.0)))
                    parts.append(jnp.clip(diff[:, b * 128 : (b + 1) * 128], -lim, lim))
                for half in range(2):
                    rr = 2 * t + half
                    packed = jnp.concatenate([p[8 * half : 8 * half + 8] for p in parts], axis=0)
                    rx = lax.rem(rr, nx)
                    rz = lax.rem(rr // nx, nz)
                    ry = rr // (nx * nz)
                    dec[rx, ry * nz + rz] = packed.astype(BF16)

            for k in range(nx - 1):
                x_sum(k).start()

            if nz > 1:

                @pl.when(leader)
                def _():
                    all_groups()

        @pl.when(due(0, t))
        def _():
            for k in range(nx - 1):
                x_sum(k).wait_recv()

            @pl.loop(0, ny * nz)
            def _(g):
                total = dec[x, g].astype(F32)
                for k in range(nx - 1):
                    total += got1[k, g].astype(F32)
                part2[g // nz, lax.rem(g, nz)] = total

            for k in range(ny - 1):
                y_sum(k).start()

        @pl.when(due(1, t))
        def _():
            for k in range(ny - 1):
                y_sum(k).wait_recv()
            for g in range(nz):
                total = part2[y, g]
                for k in range(ny - 1):
                    total += got2[k, g]
                part3[g] = total

            if nz > 1:

                @pl.when(jnp.logical_not(leader))
                def _():
                    pl.semaphore_wait(tok_go, 1)

                for k in range(2):
                    z_far(k).start()

        @pl.when(due(2, t))
        def _():
            if nz > 1:
                for k in range(2):
                    z_far(k).wait_recv()
                    to = lax.rem(z + (1, nz - 1)[k], nz)
                    part3[to, half[k]] += far3[k]
                for k in range(2):
                    z_sum(k).start()

        @pl.when(due(3, t))
        def _():
            total = part3[z]
            if nz > 1:
                for k in range(2):
                    z_sum(k).wait_recv()
                    total += got3[k]
            average = total / replicas
            m_copy.wait()
            mom_now = mom_v[...]
            mom_p = jnp.concatenate([mom_now[:, b * 128 : (b + 1) * 128] for b in range(4)], axis=0)
            mom_next = 0.9 * mom_p + average
            own = glob_v[pl.ds(pl.multiple_of(r // 2 * 16, 16), 16), :].astype(F32)
            own = jnp.where(lax.rem(r, 2) == 0, own[0:8], own[8:16])
            own_p = jnp.concatenate([own[:, b * 128 : (b + 1) * 128] for b in range(4)], axis=0)
            gath[x, y, z] = (own_p - 0.7 * (0.9 * mom_next + average)).astype(BF16)
            if nz > 1:
                for k in range(2):
                    z_gather(k, z).start()
            for b in range(4):
                mn_v[:, b * 128 : (b + 1) * 128] = mom_next[8 * b : 8 * b + 8]

        @pl.when(due(4, t))
        def _():
            if nz > 1:
                for k in range(2):
                    before = lax.rem(z + (nz - 1, 1)[k], nz)
                    z_gather(k, before).wait_recv()
                    z_pass(k, before).start()

        @pl.when(due(5, t))
        def _():
            if nz > 1:
                for k in range(2):
                    z_pass(k, lax.rem(z + 2, nz)).wait_recv()
            for k in range(ny - 1):
                y_gather(k, y).start()

        @pl.when(due(6, t))
        def _():
            for k in range(ny - 1):
                y_gather(k, lax.rem(y + ny - k - 1, ny)).wait_recv()
            for k in range(nx - 1):
                x_gather(k, x).start()

        @pl.when(due(7, t))
        def _():
            for k in range(nx - 1):
                x_gather(k, lax.rem(x + nx - k - 1, nx)).wait_recv()

            @pl.loop(0, BLK // 16)
            def _(n):
                halves = []
                for half in range(2):
                    rr = 2 * n + half
                    piece = gath[lax.rem(rr, nx), rr // (nx * nz), lax.rem(rr // nx, nz)].astype(F32)
                    halves.append(
                        jnp.concatenate([piece[8 * b : 8 * b + 8] for b in range(4)], axis=1)
                    )
                gn_v[pl.ds(pl.multiple_of(n * 16, 16), 16), :] = jnp.concatenate(
                    halves, axis=0
                ).astype(BF16)


    @pl.loop(0, NC)
    def _(p):
        q, h = p // NH, lax.rem(p, NH)
        n = i * NC + p
        share(i, q, h, is_next, CHIPS - 2)

        @pl.when(i <= CHIPS - 3)
        def _():
            dn_copy(n).wait_recv()
            acc[...] += dn_buf[n].astype(F32)

        @pl.when(i >= 2)
        def _():
            up_copy(n).wait_recv()
            acc[...] += up_buf[n].astype(F32)

        rows = pl.ds(pl.multiple_of(q * QR, QR), QR)
        kv = pl.ds(pl.multiple_of(h * HC, HC), HC)
        stepped = inner_v[rows, kv].astype(F32) - 0.5 * acc[...]
        out_v[rows, kv] = (0.5 * stepped + 0.5 * gn_v[rows, kv].astype(F32)).astype(BF16)

    sc_copy.wait_send()

    @pl.loop(0, CHIPS)
    def _(d):
        st_copy(d).wait_send()

    @pl.when(is_next)
    def _():
        for h in range(2):
            cx_forward(h).wait_send()

    @pl.when(is_end)
    def _():
        for h in range(2):
            cx_copy(h).wait_send()
        for other in range(2):
            whole = t_ext.at[0:TOK, 0 : (CHIPS - 1) * BLK]
            pltpu.make_async_copy(whole, whole, tx_send.at[other]).wait()

    def wait_block(buf, sem, d):
        whole = buf.at[pl.ds(d * NC, NC)]
        pltpu.make_async_copy(whole, whole, sem.at[d]).wait()

    @pl.loop(0, CHIPS)
    def _(d):
        @pl.when((i >= 1) & (d > i))
        def _():
            wait_block(up_buf, up_send, d)

        @pl.when((i <= CHIPS - 2) & (d < i))
        def _():
            wait_block(dn_buf, dn_send, d)

    for k in range(nx - 1):
        x_sum(k).wait_send()
        x_gather(k, x).wait_send()
    for k in range(ny - 1):
        y_sum(k).wait_send()
        y_gather(k, y).wait_send()
    if nz > 1:
        for k in range(2):
            z_far(k).wait_send()
            z_sum(k).wait_send()
            z_gather(k, z).wait_send()
            z_pass(k, lax.rem(z + (nz - 1, 1)[k], nz)).wait_send()


def store(a, b, c, a_out, b_out, c_out, sems):
    copies = [
        pltpu.make_async_copy(src, dst, sems.at[k])
        for k, (src, dst) in enumerate(((a, a_out), (b, b_out), (c, c_out)))
    ]
    for copy in copies:
        copy.start()
    for copy in copies:
        copy.wait()


def body(dims, tokens, cotangent, inner_weights, global_weights, momentum, exponents):
    ny, nz, nx = dims
    replicas = ny * nz * nx
    anywhere = pl.BlockSpec(memory_space=pl.ANY)
    sem = pltpu.SemaphoreType.DMA
    blended, gnext, mnext = pl.pallas_call(
        functools.partial(kernel, dims, replicas),
        out_shape=(
            pltpu.VMEM((BLK, BLK), BF16),
            pltpu.VMEM((BLK, BLK), BF16),
            pltpu.VMEM((8, BLK), F32),
        ),
        in_specs=[anywhere] * 5 + [pl.BlockSpec(memory_space=pltpu.SMEM)],
        out_specs=(pl.BlockSpec(memory_space=pltpu.VMEM),) * 3,
        scratch_shapes=[
            pltpu.VMEM((2 * TOK, CHIPS * BLK), BF16),
            pltpu.VMEM((2 * TOK, CHIPS * BLK), BF16),
            pltpu.VMEM((2 * TOK, BLK), BF16),
            pltpu.VMEM((2 * TOK, BLK), BF16),
            pltpu.VMEM((CHIPS * NC, QR, HC), BF16),
            pltpu.VMEM((CHIPS * NC, QR, HC), BF16),
            pltpu.VMEM((QR, HC), F32),
            pltpu.VMEM((BLK, BLK), BF16),
            pltpu.VMEM((BLK, BLK), BF16),
            pltpu.VMEM((8, BLK), F32),
            pltpu.VMEM((nx, 64 // nx, 32, 128), BF16),
            pltpu.VMEM((3, ny * nz, 32, 128), BF16),
            pltpu.VMEM((ny, nz, 32, 128), F32),
            pltpu.VMEM((3, nz, 32, 128), F32),
            pltpu.VMEM((nz, 32, 128), F32),
            pltpu.VMEM((2, 16, 128), F32),
            pltpu.VMEM((2, 32, 128), F32),
            pltpu.VMEM((nx, 64 // (nx * nz), nz, 32, 128), BF16),
            sem((4,)),
            sem((CHIPS,)),
            sem((CHIPS + 1,)),
            sem((CHIPS + 1,)),
            sem((4,)),
            sem((4,)),
            sem((2,)),
            sem((NQ + CHIPS - 2, 2)),
            sem((CHIPS,)),
            sem((CHIPS * NC,)),
            sem((CHIPS,)),
            sem((CHIPS * NC,)),
            sem((8, 3)),
            sem((8, 3)),
            pltpu.SemaphoreType.REGULAR,
        ],
        compiler_params=pltpu.CompilerParams(
            collective_id=0, has_side_effects=True, vmem_limit_bytes=62 << 20
        ),
    )(tokens, cotangent, inner_weights[0], global_weights, momentum, jnp.swapaxes(exponents[0], 0, 1))
    blended, gnext, mnext = pl.pallas_call(
        store,
        out_shape=(
            jax.ShapeDtypeStruct((BLK, BLK), BF16),
            jax.ShapeDtypeStruct((BLK, BLK), BF16),
            jax.ShapeDtypeStruct((8, BLK), F32),
        ),
        in_specs=[anywhere] * 3,
        out_specs=(anywhere,) * 3,
        scratch_shapes=[sem((3,))],
        compiler_params=pltpu.CompilerParams(vmem_limit_bytes=1 << 20),
    )(blended, gnext, mnext)
    return blended[None], gnext, mnext


def solution(mesh):
    return jax.shard_map(
        functools.partial(body, (4, 4, 4)),
        mesh=mesh,
        in_specs=(
            P(("replica", "fsdp"), None),
            P(("replica", "fsdp"), None),
            P("replica", "fsdp", None),
            P("fsdp", None),
            P(("fsdp", "replica"), None),
            P("replica", "fsdp", None),
        ),
        out_specs=(P("replica", "fsdp", None), P("fsdp", None), P(("fsdp", "replica"), None)),
        check_vma=False,
    )
```

```python
import functools

import jax
import jax.numpy as jnp
from jax import lax
from jax.experimental import pallas as pl
from jax.experimental.pallas import tpu as pltpu
from jax.sharding import PartitionSpec as P

MESH = pl.DeviceIdType.MESH
F32 = jnp.float32
BF16 = jnp.bfloat16

CHIPS = 8
TOK = 128
BLK = 512
QR = 128
HC = 512
NQ = BLK // QR
NH = BLK // HC
NC = NQ * NH
LAG = 3
DECODE = 1
DEPTH = 1
STAGES = (
    (4, 4, 4, 4),
    (8, 6, 5, 6),
    (13, 10, 9, 10),
    (15, 12, 12, 12),
    (18, 15, 15, 15),
    (20, 17, 17, 17),
    (22, 20, 20, 20),
)


def kernel(
    dims,
    replicas,
    tok,
    cot,
    inner,
    glob,
    mom,
    expo,
    out_v,
    gn_v,
    mn_v,
    t_own,
    t_ext,
    c_own,
    c_ext,
    up_buf,
    dn_buf,
    acc,
    inner_v,
    glob_v,
    mom_v,
    dec,
    got1,
    part2,
    got2,
    part3,
    far3,
    got3,
    gath,
    in_sem,
    tin_sem,
    sib_send,
    sib_recv,
    cx_send,
    cx_recv,
    tx_send,
    tx_recv,
    up_send,
    up_recv,
    dn_send,
    dn_recv,
    st_send,
    st_recv,
    tok_go,
):
    ny, nz, nx = dims
    r = lax.axis_index("replica")
    f = lax.axis_index("fsdp")
    i = f // 2
    c = lax.rem(f, 2)
    x = lax.rem(r, nx)
    z = lax.rem(r // nx, nz)
    y = r // (nx * nz)
    sib = (r, f + 1 - 2 * c)
    low_end, high_end = i == 0, i == CHIPS - 1
    is_end = low_end | high_end
    is_next = (i == 1) | (i == CHIPS - 2)
    paired = is_end | is_next
    mate_i = i + 1 - 2 * lax.rem(i, 2)
    mate = (r, 2 * mate_i + c)
    cross = (r, 2 * mate_i + 1 - c)
    above = (r, jnp.minimum(f + 2, 2 * CHIPS - 1))
    below = (r, jnp.maximum(f - 2, 0))

    def at(yy, zz, xx):
        return ((yy * nz + zz) * nx + xx, f)

    x_peers = [at(y, z, lax.rem(x + k, nx)) for k in range(1, nx)]
    y_peers = [at(lax.rem(y + k, ny), z, x) for k in range(1, ny)]

    def t_copy(d):
        return pltpu.make_async_copy(
            tok.at[:, pl.ds(pl.multiple_of((2 * d + c) * BLK, BLK), BLK)],
            t_own.at[0:TOK, pl.ds(pl.multiple_of(d * BLK, BLK), BLK)],
            tin_sem.at[d],
        )

    c_copy = pltpu.make_async_copy(cot, c_own.at[0:TOK], in_sem.at[0])
    i_copy = pltpu.make_async_copy(inner, inner_v, in_sem.at[1])
    g_copy = pltpu.make_async_copy(glob, glob_v, in_sem.at[2])
    m_copy = pltpu.make_async_copy(mom, mom_v, in_sem.at[3])
    i_copy.start()
    g_copy.start()
    c_copy.start()
    m_copy.start()

    @pl.loop(0, CHIPS)
    def _(d):
        t_copy(d).start()

    root = min(2, nz - 1)
    leader_i = jnp.where((z == root) & (nz > 1), CHIPS // 2 - 1, CHIPS - 1)
    leader = i == leader_i
    line = [(r, lax.rem(f + 2 * k, 2 * CHIPS)) for k in range(1, CHIPS)]

    def at_z(zz):
        return at(y, zz, x)

    def signal(semaphore, peer):
        pl.semaphore_signal(semaphore, 1, device_id=peer, device_id_type=MESH)

    barrier = pltpu.get_barrier_semaphore()
    for peer in [sib] + x_peers + y_peers:
        signal(barrier, peer)

    @pl.when(i < CHIPS - 1)
    def _():
        signal(barrier, above)

    @pl.when(i > 0)
    def _():
        signal(barrier, below)

    @pl.when(paired)
    def _():
        signal(barrier, cross)

    @pl.when((i < leader_i - 1) | (i > leader_i + 1))
    def _():
        signal(barrier, (r, 2 * leader_i + c))

    near = jnp.where(leader, CHIPS - 1 + jnp.where(z == root, nz - 1, 0), jnp.where(is_end, 1, 2))
    pl.semaphore_wait(barrier, 1 + (nx - 1) + (ny - 1) + near + jnp.where(paired, 1, 0))

    if nz > 1:

        @pl.when(leader & (z != root))
        def _():
            signal(barrier, (at_z(root)[0], 2 * (CHIPS // 2 - 1) + c))

    def all_groups():
        @pl.when(z == root)
        def _():
            for k in range(1, nz):
                signal(tok_go, (at_z(lax.rem(z + k, nz))[0], 2 * (CHIPS - 1) + c))

        @pl.when(z != root)
        def _():
            pl.semaphore_wait(tok_go, 1)

        for peer in line:
            signal(tok_go, peer)

    if nz > 1:

        @pl.when(leader & (z == root))
        def _():
            all_groups()

    def cx_copy(h):
        cols = slice(h * 256, h * 256 + 256)
        return pltpu.make_async_remote_copy(
            cot.at[:, cols],
            c_ext.at[0:TOK, cols],
            cx_send.at[h],
            cx_recv.at[h],
            device_id=mate,
            device_id_type=MESH,
        )

    def cx_forward(h):
        cols = slice(h * 256, h * 256 + 256)
        return pltpu.make_async_remote_copy(
            c_ext.at[0:TOK, cols],
            c_ext.at[TOK : 2 * TOK, cols],
            cx_send.at[2 + h],
            cx_recv.at[2 + h],
            device_id=sib,
            device_id_type=MESH,
        )

    def tx_copy(k, q, width, n, other):
        d = jnp.where((i == 0) | (i == 1), CHIPS - 1 - k, k)
        src_c = (1 - c) if other else c
        return pltpu.make_async_remote_copy(
            tok.at[:, pl.ds(pl.multiple_of((2 * d + src_c) * BLK + q * QR, QR), width)],
            t_ext.at[
                (TOK if other else 0) : (2 * TOK if other else TOK),
                pl.ds(pl.multiple_of(d * BLK + q * QR, QR), width),
            ],
            tx_send.at[1 if other else 0],
            tx_recv.at[n, 1 if other else 0],
            device_id=cross if other else mate,
            device_id_type=MESH,
        )

    def tx_part(q, other):
        return tx_copy(0, q, QR, q, other)

    def tx_whole(k, other):
        return tx_copy(k, 0, BLK, NQ - 1 + k, other)

    @pl.when(is_end)
    def _():
        cx_copy(0).start()
        tx_part(0, False).start()
        tx_part(0, True).start()
        cx_copy(1).start()

        @pl.loop(1, NQ)
        def _(q):
            tx_part(q, False).start()
            tx_part(q, True).start()

    def tx_next(*blocks):
        @pl.when(is_end)
        def _():
            for k in blocks:
                tx_whole(k, False).start()
                tx_whole(k, True).start()

    sc_copy = pltpu.make_async_remote_copy(
        cot,
        c_own.at[TOK : 2 * TOK],
        sib_send.at[CHIPS],
        sib_recv.at[CHIPS],
        device_id=sib,
        device_id_type=MESH,
    )

    def st_copy(d):
        return pltpu.make_async_remote_copy(
            tok.at[:, pl.ds(pl.multiple_of((2 * d + 1 - c) * BLK, BLK), BLK)],
            t_own.at[TOK : 2 * TOK, pl.ds(pl.multiple_of(d * BLK, BLK), BLK)],
            sib_send.at[d],
            sib_recv.at[d],
            device_id=sib,
            device_id_type=MESH,
        )

    sc_copy.start()

    @pl.loop(0, CHIPS)
    def _(d):
        st_copy(d).start()

    def stage_copy(stage, k, src, dst, peer):
        return pltpu.make_async_remote_copy(
            src, dst, st_send.at[stage, k], st_recv.at[stage, k], device_id=peer, device_id_type=MESH
        )

    def x_sum(k):
        return stage_copy(0, k, dec.at[lax.rem(x + k + 1, nx)], got1.at[k], x_peers[k])

    def y_sum(k):
        return stage_copy(1, k, part2.at[lax.rem(y + k + 1, ny)], got2.at[k], y_peers[k])

    z_next = [at_z(lax.rem(z + 1, nz)), at_z(lax.rem(z + nz - 1, nz))]
    half = [slice(0, 16), slice(16, 32)]

    def z_far(k):
        src = part3.at[lax.rem(z + 2, nz), half[k]]
        return stage_copy(2, k, src, far3.at[k], z_next[k])

    def z_sum(k):
        src = part3.at[lax.rem(z + (1, nz - 1)[k], nz)]
        return stage_copy(3, k, src, got3.at[k], z_next[k])

    def z_gather(k, zz):
        ref = gath.at[x, y, zz]
        return stage_copy(4, k, ref, ref, at_z(lax.rem(z + k + 1, nz)))

    def y_gather(k, yy):
        ref = gath.at[x, yy]
        return stage_copy(5, k, ref, ref, y_peers[k])

    def x_gather(k, xx):
        ref = gath.at[xx]
        return stage_copy(6, k, ref, ref, x_peers[k])

    @pl.when(is_next)
    def _():
        for h in range(2):
            cx_copy(h).wait_recv()
            cx_forward(h).start()

    def t_wait(d):
        t_copy(d).wait()
        st_copy(d).wait_recv()

    c_copy.wait()
    sc_copy.wait_recv()
    t_wait(CHIPS - 1)
    t_wait(0)

    @pl.when(is_next)
    def _():
        for h in range(2):
            cx_forward(h).wait_recv()

    def share(d, q, h, extra, k):
        cols = pl.ds(pl.multiple_of(d * BLK + q * QR, QR), QR)
        kv = pl.ds(pl.multiple_of(h * HC, HC), HC)
        contract = (((0,), (0,)), ((), ()))
        acc[...] = lax.dot_general(
            t_own[:, cols], c_own[:, kv], contract, preferred_element_type=F32
        )

        @pl.when(extra)
        def _():
            @pl.when((h == 0) & (k == 0))
            def _():
                tx_part(q, False).wait_recv()
                tx_part(q, True).wait_recv()

            @pl.when((h == 0) & (q == 0) & (k > 0))
            def _():
                tx_whole(k, False).wait_recv()
                tx_whole(k, True).wait_recv()

            acc[...] += lax.dot_general(
                t_ext[:, cols], c_ext[:, kv], contract, preferred_element_type=F32
            )

    def up_copy(n):
        return pltpu.make_async_remote_copy(
            up_buf.at[n], up_buf.at[n], up_send.at[n], up_recv.at[n], device_id=above, device_id_type=MESH
        )

    def dn_copy(n):
        return pltpu.make_async_remote_copy(
            dn_buf.at[n], dn_buf.at[n], dn_send.at[n], dn_recv.at[n], device_id=below, device_id_type=MESH
        )

    def due(stage, t):
        when = STAGES[stage][0]
        for group in range(1, 4):
            when = jnp.where(z == group, STAGES[stage][group], when)
        return t == when

    ticks = (CHIPS - 2) * NC

    @pl.loop(0, ticks)
    def _(t):
        su = t - (i - 1) * LAG
        ku = su // NC

        @pl.when((i >= 1) & (su >= 0) & (su < (CHIPS - 1 - i) * NC))
        def _():
            d = CHIPS - 1 - ku
            p = lax.rem(su, NC)
            n = d * NC + p
            share(d, p // NH, lax.rem(p, NH), i == 1, ku)

            @pl.when(i > 1)
            def _():
                up_copy(n).wait_recv()
                up_buf[n] = (acc[...] + up_buf[n].astype(F32)).astype(BF16)

            @pl.when(i == 1)
            def _():
                up_buf[n] = acc[...].astype(BF16)

            up_copy(n).start()

            @pl.when(su >= DEPTH)
            def _():
                before = su - DEPTH
                up_copy((CHIPS - 1 - before // NC) * NC + lax.rem(before, NC)).wait_send()

        sd = t - (CHIPS - 2 - i) * LAG
        kd = sd // NC

        @pl.when((i <= CHIPS - 2) & (sd >= 0) & (sd < i * NC))
        def _():
            p = lax.rem(sd, NC)
            n = kd * NC + p
            share(kd, p // NH, lax.rem(p, NH), i == CHIPS - 2, kd)

            @pl.when(i < CHIPS - 2)
            def _():
                dn_copy(n).wait_recv()
                dn_buf[n] = (acc[...] + dn_buf[n].astype(F32)).astype(BF16)

            @pl.when(i == CHIPS - 2)
            def _():
                dn_buf[n] = acc[...].astype(BF16)

            dn_copy(n).start()

            @pl.when(sd >= DEPTH)
            def _():
                dn_copy(sd - DEPTH).wait_send()

        @pl.when(t == DECODE)
        def _():
            @pl.loop(1, CHIPS - 1)
            def _(d):
                t_wait(d)

            i_copy.wait()
            g_copy.wait()

            @pl.loop(0, BLK // 16)
            def _(t):
                rows = pl.ds(pl.multiple_of(t * 16, 16), 16)
                diff = glob_v[rows, :].astype(F32) - inner_v[rows, :].astype(F32)
                parts = []
                for b in range(4):
                    e = expo[b, t // 2]
                    lim = jnp.where(e < 0, 1.0, jnp.where(e == 0, 2.0, jnp.where(e == 1, 4.0, 8.0)))
                    parts.append(jnp.clip(diff[:, b * 128 : (b + 1) * 128], -lim, lim))
                for half in range(2):
                    rr = 2 * t + half
                    packed = jnp.concatenate([p[8 * half : 8 * half + 8] for p in parts], axis=0)
                    rx = lax.rem(rr, nx)
                    rz = lax.rem(rr // nx, nz)
                    ry = rr // (nx * nz)
                    dec[rx, ry * nz + rz] = packed.astype(BF16)

            for k in range(nx - 1):
                x_sum(k).start()
            tx_next(1, 2)

            if nz > 1:

                @pl.when(leader & (z != root))
                def _():
                    all_groups()

        @pl.when(due(0, t))
        def _():
            for k in range(nx - 1):
                x_sum(k).wait_recv()

            @pl.loop(0, ny * nz)
            def _(g):
                total = dec[x, g].astype(F32)
                for k in range(nx - 1):
                    total += got1[k, g].astype(F32)
                part2[g // nz, lax.rem(g, nz)] = total

            for k in range(ny - 1):
                y_sum(k).start()
            tx_next(3)

        @pl.when(due(1, t))
        def _():
            for k in range(ny - 1):
                y_sum(k).wait_recv()
            for g in range(nz):
                total = part2[y, g]
                for k in range(ny - 1):
                    total += got2[k, g]
                part3[g] = total

            if nz > 1:

                @pl.when(jnp.logical_not(leader))
                def _():
                    pl.semaphore_wait(tok_go, 1)

                for k in range(2):
                    z_far(k).start()
            tx_next(4)

        @pl.when(due(2, t))
        def _():
            if nz > 1:
                for k in range(2):
                    z_far(k).wait_recv()
                    to = lax.rem(z + (1, nz - 1)[k], nz)
                    part3[to, half[k]] += far3[k]
                for k in range(2):
                    z_sum(k).start()
            tx_next(5)

        @pl.when(due(3, t))
        def _():
            total = part3[z]
            if nz > 1:
                for k in range(2):
                    z_sum(k).wait_recv()
                    total += got3[k]
            average = total / replicas
            m_copy.wait()
            mom_now = mom_v[...]
            mom_p = jnp.concatenate([mom_now[:, b * 128 : (b + 1) * 128] for b in range(4)], axis=0)
            mom_next = 0.9 * mom_p + average
            own = glob_v[pl.ds(pl.multiple_of(r // 2 * 16, 16), 16), :].astype(F32)
            own = jnp.where(lax.rem(r, 2) == 0, own[0:8], own[8:16])
            own_p = jnp.concatenate([own[:, b * 128 : (b + 1) * 128] for b in range(4)], axis=0)
            gath[x, y, z] = (own_p - 0.7 * (0.9 * mom_next + average)).astype(BF16)
            for k in range(nz - 1):
                z_gather(k, z).start()
            tx_next(6)
            for b in range(4):
                mn_v[:, b * 128 : (b + 1) * 128] = mom_next[8 * b : 8 * b + 8]

        @pl.when(due(4, t))
        def _():
            for k in range(nz - 1):
                z_gather(k, lax.rem(z + nz - k - 1, nz)).wait_recv()
            for k in range(ny - 1):
                y_gather(k, y).start()

        @pl.when(due(5, t))
        def _():
            for k in range(ny - 1):
                y_gather(k, lax.rem(y + ny - k - 1, ny)).wait_recv()
            for k in range(nx - 1):
                x_gather(k, x).start()

        @pl.when(due(6, t))
        def _():
            for k in range(nx - 1):
                x_gather(k, lax.rem(x + nx - k - 1, nx)).wait_recv()

            @pl.loop(0, BLK // 16)
            def _(n):
                halves = []
                for half in range(2):
                    rr = 2 * n + half
                    piece = gath[lax.rem(rr, nx), rr // (nx * nz), lax.rem(rr // nx, nz)].astype(F32)
                    halves.append(
                        jnp.concatenate([piece[8 * b : 8 * b + 8] for b in range(4)], axis=1)
                    )
                gn_v[pl.ds(pl.multiple_of(n * 16, 16), 16), :] = jnp.concatenate(
                    halves, axis=0
                ).astype(BF16)


    @pl.loop(0, NC)
    def _(p):
        q, h = p // NH, lax.rem(p, NH)
        n = i * NC + p
        share(i, q, h, is_next, CHIPS - 2)

        @pl.when(i <= CHIPS - 3)
        def _():
            dn_copy(n).wait_recv()
            acc[...] += dn_buf[n].astype(F32)

        @pl.when(i >= 2)
        def _():
            up_copy(n).wait_recv()
            acc[...] += up_buf[n].astype(F32)

        rows = pl.ds(pl.multiple_of(q * QR, QR), QR)
        kv = pl.ds(pl.multiple_of(h * HC, HC), HC)
        stepped = inner_v[rows, kv].astype(F32) - 0.5 * acc[...]
        out_v[rows, kv] = (0.5 * stepped + 0.5 * gn_v[rows, kv].astype(F32)).astype(BF16)

    sc_copy.wait_send()

    @pl.loop(0, CHIPS)
    def _(d):
        st_copy(d).wait_send()

    @pl.when(is_next)
    def _():
        for h in range(2):
            cx_forward(h).wait_send()

    @pl.when(is_end)
    def _():
        for h in range(2):
            cx_copy(h).wait_send()
        for other in range(2):
            whole = t_ext.at[0:TOK, 0 : (CHIPS - 1) * BLK]
            pltpu.make_async_copy(whole, whole, tx_send.at[other]).wait()

    for k in range(NC - DEPTH, NC):

        @pl.when((i >= 1) & (i < CHIPS - 1))
        def _(k=k):
            up_copy((i + 1) * NC + k).wait_send()
            dn_copy((i - 1) * NC + k).wait_send()

    for k in range(nx - 1):
        x_sum(k).wait_send()
        x_gather(k, x).wait_send()
    for k in range(ny - 1):
        y_sum(k).wait_send()
        y_gather(k, y).wait_send()
    if nz > 1:
        for k in range(2):
            z_far(k).wait_send()
            z_sum(k).wait_send()
    for k in range(nz - 1):
        z_gather(k, z).wait_send()


def store(a, b, c, a_out, b_out, c_out, sems):
    copies = [
        pltpu.make_async_copy(src, dst, sems.at[k])
        for k, (src, dst) in enumerate(((a, a_out), (b, b_out), (c, c_out)))
    ]
    for copy in copies:
        copy.start()
    for copy in copies:
        copy.wait()


def body(dims, tokens, cotangent, inner_weights, global_weights, momentum, exponents):
    ny, nz, nx = dims
    replicas = ny * nz * nx
    anywhere = pl.BlockSpec(memory_space=pl.ANY)
    sem = pltpu.SemaphoreType.DMA
    blended, gnext, mnext = pl.pallas_call(
        functools.partial(kernel, dims, replicas),
        out_shape=(
            pltpu.VMEM((BLK, BLK), BF16),
            pltpu.VMEM((BLK, BLK), BF16),
            pltpu.VMEM((8, BLK), F32),
        ),
        in_specs=[anywhere] * 5 + [pl.BlockSpec(memory_space=pltpu.SMEM)],
        out_specs=(pl.BlockSpec(memory_space=pltpu.VMEM),) * 3,
        scratch_shapes=[
            pltpu.VMEM((2 * TOK, CHIPS * BLK), BF16),
            pltpu.VMEM((2 * TOK, CHIPS * BLK), BF16),
            pltpu.VMEM((2 * TOK, BLK), BF16),
            pltpu.VMEM((2 * TOK, BLK), BF16),
            pltpu.VMEM((CHIPS * NC, QR, HC), BF16),
            pltpu.VMEM((CHIPS * NC, QR, HC), BF16),
            pltpu.VMEM((QR, HC), F32),
            pltpu.VMEM((BLK, BLK), BF16),
            pltpu.VMEM((BLK, BLK), BF16),
            pltpu.VMEM((8, BLK), F32),
            pltpu.VMEM((nx, 64 // nx, 32, 128), BF16),
            pltpu.VMEM((3, ny * nz, 32, 128), BF16),
            pltpu.VMEM((ny, nz, 32, 128), F32),
            pltpu.VMEM((3, nz, 32, 128), F32),
            pltpu.VMEM((nz, 32, 128), F32),
            pltpu.VMEM((2, 16, 128), F32),
            pltpu.VMEM((2, 32, 128), F32),
            pltpu.VMEM((nx, 64 // (nx * nz), nz, 32, 128), BF16),
            sem((4,)),
            sem((CHIPS,)),
            sem((CHIPS + 1,)),
            sem((CHIPS + 1,)),
            sem((4,)),
            sem((4,)),
            sem((2,)),
            sem((NQ + CHIPS - 2, 2)),
            sem((CHIPS * NC,)),
            sem((CHIPS * NC,)),
            sem((CHIPS * NC,)),
            sem((CHIPS * NC,)),
            sem((7, 3)),
            sem((7, 3)),
            pltpu.SemaphoreType.REGULAR,
        ],
        compiler_params=pltpu.CompilerParams(
            collective_id=0, has_side_effects=True, vmem_limit_bytes=62 << 20
        ),
    )(tokens, cotangent, inner_weights[0], global_weights, momentum, jnp.swapaxes(exponents[0], 0, 1))
    blended, gnext, mnext = pl.pallas_call(
        store,
        out_shape=(
            jax.ShapeDtypeStruct((BLK, BLK), BF16),
            jax.ShapeDtypeStruct((BLK, BLK), BF16),
            jax.ShapeDtypeStruct((8, BLK), F32),
        ),
        in_specs=[anywhere] * 3,
        out_specs=(anywhere,) * 3,
        scratch_shapes=[sem((3,))],
        compiler_params=pltpu.CompilerParams(vmem_limit_bytes=1 << 20),
    )(blended, gnext, mnext)
    return blended[None], gnext, mnext


def solution(mesh):
    return jax.shard_map(
        functools.partial(body, (4, 4, 4)),
        mesh=mesh,
        in_specs=(
            P(("replica", "fsdp"), None),
            P(("replica", "fsdp"), None),
            P("replica", "fsdp", None),
            P("fsdp", None),
            P(("fsdp", "replica"), None),
            P("replica", "fsdp", None),
        ),
        out_specs=(P("replica", "fsdp", None), P("fsdp", None), P(("fsdp", "replica"), None)),
        check_vma=False,
    )
```

```python
import functools

import jax
import jax.numpy as jnp
from jax import lax
from jax.experimental import pallas as pl
from jax.experimental.pallas import tpu as pltpu
from jax.sharding import PartitionSpec as P

MESH = pl.DeviceIdType.MESH
F32 = jnp.float32
BF16 = jnp.bfloat16

CHIPS = 8
TOK = 128
BLK = 512
QR = 128
HC = 512
NQ = BLK // QR
NH = BLK // HC
NC = NQ * NH
LAG = 3
DECODE = 1
DEPTH = 1
STAGES = (
    (4, 4, 4, 4),
    (8, 6, 6, 6),
    (12, 9, 9, 9),
    (15, 12, 12, 12),
    (18, 16, 15, 16),
    (20, 18, 17, 18),
    (23, 21, 20, 21),
)


def kernel(
    dims,
    replicas,
    tok,
    cot,
    inner,
    glob,
    mom,
    expo,
    out_v,
    gn_v,
    mn_v,
    t_own,
    t_ext,
    c_own,
    c_ext,
    up_buf,
    dn_buf,
    acc,
    inner_v,
    glob_v,
    mom_v,
    dec,
    got1,
    part2,
    got2,
    part3,
    far3,
    got3,
    gath,
    in_sem,
    tin_sem,
    sib_send,
    sib_recv,
    cx_send,
    cx_recv,
    tx_send,
    tx_recv,
    up_send,
    up_recv,
    dn_send,
    dn_recv,
    st_send,
    st_recv,
    tok_go,
):
    ny, nz, nx = dims
    r = lax.axis_index("replica")
    f = lax.axis_index("fsdp")
    i = f // 2
    c = lax.rem(f, 2)
    x = lax.rem(r, nx)
    z = lax.rem(r // nx, nz)
    y = r // (nx * nz)
    sib = (r, f + 1 - 2 * c)
    low_end, high_end = i == 0, i == CHIPS - 1
    is_end = low_end | high_end
    is_next = (i == 1) | (i == CHIPS - 2)
    paired = is_end | is_next
    mate_i = i + 1 - 2 * lax.rem(i, 2)
    mate = (r, 2 * mate_i + c)
    cross = (r, 2 * mate_i + 1 - c)
    above = (r, jnp.minimum(f + 2, 2 * CHIPS - 1))
    below = (r, jnp.maximum(f - 2, 0))

    def at(yy, zz, xx):
        return ((yy * nz + zz) * nx + xx, f)

    x_peers = [at(y, z, lax.rem(x + k, nx)) for k in range(1, nx)]
    y_peers = [at(lax.rem(y + k, ny), z, x) for k in range(1, ny)]

    def t_copy(d):
        return pltpu.make_async_copy(
            tok.at[:, pl.ds(pl.multiple_of((2 * d + c) * BLK, BLK), BLK)],
            t_own.at[0:TOK, pl.ds(pl.multiple_of(d * BLK, BLK), BLK)],
            tin_sem.at[d],
        )

    c_copy = pltpu.make_async_copy(cot, c_own.at[0:TOK], in_sem.at[0])
    i_copy = pltpu.make_async_copy(inner, inner_v, in_sem.at[1])
    g_copy = pltpu.make_async_copy(glob, glob_v, in_sem.at[2])
    m_copy = pltpu.make_async_copy(mom, mom_v, in_sem.at[3])
    i_copy.start()
    g_copy.start()
    c_copy.start()
    m_copy.start()

    @pl.loop(0, CHIPS)
    def _(d):
        t_copy(d).start()

    root = min(2, nz - 1)
    leader_i = jnp.where((z == root) & (nz > 1), CHIPS // 2 - 1, CHIPS - 1)
    leader = i == leader_i
    line = [(r, lax.rem(f + 2 * k, 2 * CHIPS)) for k in range(1, CHIPS)]

    def at_z(zz):
        return at(y, zz, x)

    def signal(semaphore, peer):
        pl.semaphore_signal(semaphore, 1, device_id=peer, device_id_type=MESH)

    barrier = pltpu.get_barrier_semaphore()
    for peer in [sib] + x_peers + y_peers:
        signal(barrier, peer)

    @pl.when(i < CHIPS - 1)
    def _():
        signal(barrier, above)

    @pl.when(i > 0)
    def _():
        signal(barrier, below)

    @pl.when(paired)
    def _():
        signal(barrier, cross)

    @pl.when((i < leader_i - 1) | (i > leader_i + 1))
    def _():
        signal(barrier, (r, 2 * leader_i + c))

    near = jnp.where(leader, CHIPS - 1 + jnp.where(z == root, nz - 1, 0), jnp.where(is_end, 1, 2))
    pl.semaphore_wait(barrier, 1 + (nx - 1) + (ny - 1) + near + jnp.where(paired, 1, 0))

    if nz > 1:

        @pl.when(leader & (z != root))
        def _():
            signal(barrier, (at_z(root)[0], 2 * (CHIPS // 2 - 1) + c))

    def all_groups():
        @pl.when(z == root)
        def _():
            for k in range(1, nz):
                signal(tok_go, (at_z(lax.rem(z + k, nz))[0], 2 * (CHIPS - 1) + c))

        @pl.when(z != root)
        def _():
            pl.semaphore_wait(tok_go, 1)

        for peer in line:
            signal(tok_go, peer)

    if nz > 1:

        @pl.when(leader & (z == root))
        def _():
            all_groups()

    def cx_copy(h):
        cols = slice(h * 256, h * 256 + 256)
        return pltpu.make_async_remote_copy(
            cot.at[:, cols],
            c_ext.at[0:TOK, cols],
            cx_send.at[h],
            cx_recv.at[h],
            device_id=mate,
            device_id_type=MESH,
        )

    def cx_forward(h):
        cols = slice(h * 256, h * 256 + 256)
        return pltpu.make_async_remote_copy(
            c_ext.at[0:TOK, cols],
            c_ext.at[TOK : 2 * TOK, cols],
            cx_send.at[2 + h],
            cx_recv.at[2 + h],
            device_id=sib,
            device_id_type=MESH,
        )

    def tx_copy(k, q, width, n, other):
        d = jnp.where((i == 0) | (i == 1), CHIPS - 1 - k, k)
        src_c = (1 - c) if other else c
        return pltpu.make_async_remote_copy(
            tok.at[:, pl.ds(pl.multiple_of((2 * d + src_c) * BLK + q * QR, QR), width)],
            t_ext.at[
                (TOK if other else 0) : (2 * TOK if other else TOK),
                pl.ds(pl.multiple_of(d * BLK + q * QR, QR), width),
            ],
            tx_send.at[1 if other else 0],
            tx_recv.at[n, 1 if other else 0],
            device_id=cross if other else mate,
            device_id_type=MESH,
        )

    def tx_part(q, other):
        return tx_copy(0, q, QR, q, other)

    def tx_whole(k, other):
        return tx_copy(k, 0, BLK, NQ - 1 + k, other)

    @pl.when(is_end)
    def _():
        cx_copy(0).start()
        tx_part(0, False).start()
        tx_part(0, True).start()
        cx_copy(1).start()

        @pl.loop(1, NQ)
        def _(q):
            tx_part(q, False).start()
            tx_part(q, True).start()

    def tx_next(*blocks):
        @pl.when(is_end)
        def _():
            for k in blocks:
                tx_whole(k, False).start()
                tx_whole(k, True).start()

    sc_copy = pltpu.make_async_remote_copy(
        cot,
        c_own.at[TOK : 2 * TOK],
        sib_send.at[CHIPS],
        sib_recv.at[CHIPS],
        device_id=sib,
        device_id_type=MESH,
    )

    def st_copy(d):
        return pltpu.make_async_remote_copy(
            tok.at[:, pl.ds(pl.multiple_of((2 * d + 1 - c) * BLK, BLK), BLK)],
            t_own.at[TOK : 2 * TOK, pl.ds(pl.multiple_of(d * BLK, BLK), BLK)],
            sib_send.at[d],
            sib_recv.at[d],
            device_id=sib,
            device_id_type=MESH,
        )

    sc_copy.start()

    @pl.loop(0, CHIPS)
    def _(d):
        st_copy(d).start()

    def stage_copy(stage, k, src, dst, peer):
        return pltpu.make_async_remote_copy(
            src, dst, st_send.at[stage, k], st_recv.at[stage, k], device_id=peer, device_id_type=MESH
        )

    def x_sum(k):
        return stage_copy(0, k, dec.at[lax.rem(x + k + 1, nx)], got1.at[k], x_peers[k])

    def y_sum(k):
        return stage_copy(1, k, part2.at[lax.rem(y + k + 1, ny)], got2.at[k], y_peers[k])

    z_next = [at_z(lax.rem(z + 1, nz)), at_z(lax.rem(z + nz - 1, nz))]
    half = [slice(0, 16), slice(16, 32)]

    def z_far(k):
        src = part3.at[lax.rem(z + 2, nz), half[k]]
        return stage_copy(2, k, src, far3.at[k], z_next[k])

    def z_sum(k):
        src = part3.at[lax.rem(z + (1, nz - 1)[k], nz)]
        return stage_copy(3, k, src, got3.at[k], z_next[k])

    def z_gather(k, zz):
        ref = gath.at[x, y, zz]
        return stage_copy(4, k, ref, ref, at_z(lax.rem(z + k + 1, nz)))

    def y_gather(k, yy):
        ref = gath.at[x, yy]
        return stage_copy(5, k, ref, ref, y_peers[k])

    def x_gather(k, xx):
        ref = gath.at[xx]
        return stage_copy(6, k, ref, ref, x_peers[k])

    @pl.when(is_next)
    def _():
        for h in range(2):
            cx_copy(h).wait_recv()
            cx_forward(h).start()

    def t_wait(d):
        t_copy(d).wait()
        st_copy(d).wait_recv()

    c_copy.wait()
    sc_copy.wait_recv()
    t_wait(CHIPS - 1)
    t_wait(0)

    @pl.when(is_next)
    def _():
        for h in range(2):
            cx_forward(h).wait_recv()

    def share(d, q, h, extra, k):
        cols = pl.ds(pl.multiple_of(d * BLK + q * QR, QR), QR)
        kv = pl.ds(pl.multiple_of(h * HC, HC), HC)
        contract = (((0,), (0,)), ((), ()))
        acc[...] = lax.dot_general(
            t_own[:, cols], c_own[:, kv], contract, preferred_element_type=F32
        )

        @pl.when(extra)
        def _():
            @pl.when((h == 0) & (k == 0))
            def _():
                tx_part(q, False).wait_recv()
                tx_part(q, True).wait_recv()

            @pl.when((h == 0) & (q == 0) & (k > 0))
            def _():
                tx_whole(k, False).wait_recv()
                tx_whole(k, True).wait_recv()

            acc[...] += lax.dot_general(
                t_ext[:, cols], c_ext[:, kv], contract, preferred_element_type=F32
            )

    def up_copy(n):
        return pltpu.make_async_remote_copy(
            up_buf.at[n], up_buf.at[n], up_send.at[n], up_recv.at[n], device_id=above, device_id_type=MESH
        )

    def dn_copy(n):
        return pltpu.make_async_remote_copy(
            dn_buf.at[n], dn_buf.at[n], dn_send.at[n], dn_recv.at[n], device_id=below, device_id_type=MESH
        )

    def due(stage, t):
        when = STAGES[stage][0]
        for group in range(1, 4):
            when = jnp.where(z == group, STAGES[stage][group], when)
        return t == when

    ticks = (CHIPS - 2) * NC

    @pl.loop(0, ticks)
    def _(t):
        su = t - (i - 1) * LAG
        ku = su // NC

        @pl.when((i >= 1) & (su >= 0) & (su < (CHIPS - 1 - i) * NC))
        def _():
            d = CHIPS - 1 - ku
            p = lax.rem(su, NC)
            n = d * NC + p
            share(d, p // NH, lax.rem(p, NH), i == 1, ku)

            @pl.when(i > 1)
            def _():
                up_copy(n).wait_recv()
                up_buf[n] = (acc[...] + up_buf[n].astype(F32)).astype(BF16)

            @pl.when(i == 1)
            def _():
                up_buf[n] = acc[...].astype(BF16)

            up_copy(n).start()

            @pl.when(su >= DEPTH)
            def _():
                before = su - DEPTH
                up_copy((CHIPS - 1 - before // NC) * NC + lax.rem(before, NC)).wait_send()

        sd = t - (CHIPS - 2 - i) * LAG
        kd = sd // NC

        @pl.when((i <= CHIPS - 2) & (sd >= 0) & (sd < i * NC))
        def _():
            p = lax.rem(sd, NC)
            n = kd * NC + p
            share(kd, p // NH, lax.rem(p, NH), i == CHIPS - 2, kd)

            @pl.when(i < CHIPS - 2)
            def _():
                dn_copy(n).wait_recv()
                dn_buf[n] = (acc[...] + dn_buf[n].astype(F32)).astype(BF16)

            @pl.when(i == CHIPS - 2)
            def _():
                dn_buf[n] = acc[...].astype(BF16)

            dn_copy(n).start()

            @pl.when(sd >= DEPTH)
            def _():
                dn_copy(sd - DEPTH).wait_send()

        @pl.when(t == DECODE)
        def _():
            @pl.loop(1, CHIPS - 1)
            def _(d):
                t_wait(d)

            i_copy.wait()
            g_copy.wait()

            @pl.loop(0, BLK // 16)
            def _(t):
                rows = pl.ds(pl.multiple_of(t * 16, 16), 16)
                diff = glob_v[rows, :].astype(F32) - inner_v[rows, :].astype(F32)
                parts = []
                for b in range(4):
                    e = expo[b, t // 2]
                    lim = jnp.where(e < 0, 1.0, jnp.where(e == 0, 2.0, jnp.where(e == 1, 4.0, 8.0)))
                    parts.append(jnp.clip(diff[:, b * 128 : (b + 1) * 128], -lim, lim))
                for half in range(2):
                    rr = 2 * t + half
                    packed = jnp.concatenate([p[8 * half : 8 * half + 8] for p in parts], axis=0)
                    rx = lax.rem(rr, nx)
                    rz = lax.rem(rr // nx, nz)
                    ry = rr // (nx * nz)
                    dec[rx, ry * nz + rz] = packed.astype(BF16)

            for k in range(nx - 1):
                x_sum(k).start()
            tx_next(1, 2)

            if nz > 1:

                @pl.when(leader & (z != root))
                def _():
                    all_groups()

        @pl.when(due(0, t))
        def _():
            for k in range(nx - 1):
                x_sum(k).wait_recv()

            @pl.loop(0, ny * nz)
            def _(g):
                total = dec[x, g].astype(F32)
                for k in range(nx - 1):
                    total += got1[k, g].astype(F32)
                part2[g // nz, lax.rem(g, nz)] = total

            for k in range(ny - 1):
                y_sum(k).start()
            tx_next(3)

        @pl.when(due(1, t))
        def _():
            for k in range(ny - 1):
                y_sum(k).wait_recv()
            for g in range(nz):
                total = part2[y, g]
                for k in range(ny - 1):
                    total += got2[k, g]
                part3[g] = total

            if nz > 1:

                @pl.when(jnp.logical_not(leader))
                def _():
                    pl.semaphore_wait(tok_go, 1)

                for k in range(2):
                    z_far(k).start()
            tx_next(4)

        @pl.when(due(2, t))
        def _():
            if nz > 1:
                for k in range(2):
                    z_far(k).wait_recv()
                    to = lax.rem(z + (1, nz - 1)[k], nz)
                    part3[to, half[k]] += far3[k]
                for k in range(2):
                    z_sum(k).start()
            tx_next(5)

        @pl.when(due(3, t))
        def _():
            total = part3[z]
            if nz > 1:
                for k in range(2):
                    z_sum(k).wait_recv()
                    total += got3[k]
            average = total / replicas
            m_copy.wait()
            mom_now = mom_v[...]
            mom_p = jnp.concatenate([mom_now[:, b * 128 : (b + 1) * 128] for b in range(4)], axis=0)
            mom_next = 0.9 * mom_p + average
            own = glob_v[pl.ds(pl.multiple_of(r // 2 * 16, 16), 16), :].astype(F32)
            own = jnp.where(lax.rem(r, 2) == 0, own[0:8], own[8:16])
            own_p = jnp.concatenate([own[:, b * 128 : (b + 1) * 128] for b in range(4)], axis=0)
            gath[x, y, z] = (own_p - 0.7 * (0.9 * mom_next + average)).astype(BF16)
            for k in range(nz - 1):
                z_gather(k, z).start()
            tx_next(6)
            for b in range(4):
                mn_v[:, b * 128 : (b + 1) * 128] = mom_next[8 * b : 8 * b + 8]

        @pl.when(due(4, t))
        def _():
            for k in range(nz - 1):
                z_gather(k, lax.rem(z + nz - k - 1, nz)).wait_recv()
            for k in range(ny - 1):
                y_gather(k, y).start()

        @pl.when(due(5, t))
        def _():
            for k in range(ny - 1):
                y_gather(k, lax.rem(y + ny - k - 1, ny)).wait_recv()
            for k in range(nx - 1):
                x_gather(k, x).start()

        @pl.when(due(6, t))
        def _():
            for k in range(nx - 1):
                x_gather(k, lax.rem(x + nx - k - 1, nx)).wait_recv()

            @pl.loop(0, BLK // 16)
            def _(n):
                halves = []
                for half in range(2):
                    rr = 2 * n + half
                    piece = gath[lax.rem(rr, nx), rr // (nx * nz), lax.rem(rr // nx, nz)].astype(F32)
                    halves.append(
                        jnp.concatenate([piece[8 * b : 8 * b + 8] for b in range(4)], axis=1)
                    )
                gn_v[pl.ds(pl.multiple_of(n * 16, 16), 16), :] = jnp.concatenate(
                    halves, axis=0
                ).astype(BF16)


    @pl.loop(0, NC)
    def _(p):
        q, h = p // NH, lax.rem(p, NH)
        n = i * NC + p
        share(i, q, h, is_next, CHIPS - 2)

        @pl.when(i <= CHIPS - 3)
        def _():
            dn_copy(n).wait_recv()
            acc[...] += dn_buf[n].astype(F32)

        @pl.when(i >= 2)
        def _():
            up_copy(n).wait_recv()
            acc[...] += up_buf[n].astype(F32)

        rows = pl.ds(pl.multiple_of(q * QR, QR), QR)
        kv = pl.ds(pl.multiple_of(h * HC, HC), HC)
        stepped = inner_v[rows, kv].astype(F32) - 0.5 * acc[...]
        out_v[rows, kv] = (0.5 * stepped + 0.5 * gn_v[rows, kv].astype(F32)).astype(BF16)

    sc_copy.wait_send()

    @pl.loop(0, CHIPS)
    def _(d):
        st_copy(d).wait_send()

    @pl.when(is_next)
    def _():
        for h in range(2):
            cx_forward(h).wait_send()

    @pl.when(is_end)
    def _():
        for h in range(2):
            cx_copy(h).wait_send()
        for other in range(2):
            whole = t_ext.at[0:TOK, 0 : (CHIPS - 1) * BLK]
            pltpu.make_async_copy(whole, whole, tx_send.at[other]).wait()

    for k in range(NC - DEPTH, NC):

        @pl.when((i >= 1) & (i < CHIPS - 1))
        def _(k=k):
            up_copy((i + 1) * NC + k).wait_send()
            dn_copy((i - 1) * NC + k).wait_send()

    for k in range(nx - 1):
        x_sum(k).wait_send()
        x_gather(k, x).wait_send()
    for k in range(ny - 1):
        y_sum(k).wait_send()
        y_gather(k, y).wait_send()
    if nz > 1:
        for k in range(2):
            z_far(k).wait_send()
            z_sum(k).wait_send()
    for k in range(nz - 1):
        z_gather(k, z).wait_send()


def store(a, b, c, a_out, b_out, c_out, sems):
    copies = [
        pltpu.make_async_copy(src, dst, sems.at[k])
        for k, (src, dst) in enumerate(((a, a_out), (b, b_out), (c, c_out)))
    ]
    for copy in copies:
        copy.start()
    for copy in copies:
        copy.wait()


def body(dims, tokens, cotangent, inner_weights, global_weights, momentum, exponents):
    ny, nz, nx = dims
    replicas = ny * nz * nx
    anywhere = pl.BlockSpec(memory_space=pl.ANY)
    sem = pltpu.SemaphoreType.DMA
    blended, gnext, mnext = pl.pallas_call(
        functools.partial(kernel, dims, replicas),
        out_shape=(
            pltpu.VMEM((BLK, BLK), BF16),
            pltpu.VMEM((BLK, BLK), BF16),
            pltpu.VMEM((8, BLK), F32),
        ),
        in_specs=[anywhere] * 5 + [pl.BlockSpec(memory_space=pltpu.SMEM)],
        out_specs=(pl.BlockSpec(memory_space=pltpu.VMEM),) * 3,
        scratch_shapes=[
            pltpu.VMEM((2 * TOK, CHIPS * BLK), BF16),
            pltpu.VMEM((2 * TOK, CHIPS * BLK), BF16),
            pltpu.VMEM((2 * TOK, BLK), BF16),
            pltpu.VMEM((2 * TOK, BLK), BF16),
            pltpu.VMEM((CHIPS * NC, QR, HC), BF16),
            pltpu.VMEM((CHIPS * NC, QR, HC), BF16),
            pltpu.VMEM((QR, HC), F32),
            pltpu.VMEM((BLK, BLK), BF16),
            pltpu.VMEM((BLK, BLK), BF16),
            pltpu.VMEM((8, BLK), F32),
            pltpu.VMEM((nx, 64 // nx, 32, 128), BF16),
            pltpu.VMEM((3, ny * nz, 32, 128), BF16),
            pltpu.VMEM((ny, nz, 32, 128), F32),
            pltpu.VMEM((3, nz, 32, 128), F32),
            pltpu.VMEM((nz, 32, 128), F32),
            pltpu.VMEM((2, 16, 128), F32),
            pltpu.VMEM((2, 32, 128), F32),
            pltpu.VMEM((nx, 64 // (nx * nz), nz, 32, 128), BF16),
            sem((4,)),
            sem((CHIPS,)),
            sem((CHIPS + 1,)),
            sem((CHIPS + 1,)),
            sem((4,)),
            sem((4,)),
            sem((2,)),
            sem((NQ + CHIPS - 2, 2)),
            sem((CHIPS * NC,)),
            sem((CHIPS * NC,)),
            sem((CHIPS * NC,)),
            sem((CHIPS * NC,)),
            sem((7, 3)),
            sem((7, 3)),
            pltpu.SemaphoreType.REGULAR,
        ],
        compiler_params=pltpu.CompilerParams(
            collective_id=0, has_side_effects=True, vmem_limit_bytes=62 << 20
        ),
    )(tokens, cotangent, inner_weights[0], global_weights, momentum, jnp.swapaxes(exponents[0], 0, 1))
    blended, gnext, mnext = pl.pallas_call(
        store,
        out_shape=(
            jax.ShapeDtypeStruct((BLK, BLK), BF16),
            jax.ShapeDtypeStruct((BLK, BLK), BF16),
            jax.ShapeDtypeStruct((8, BLK), F32),
        ),
        in_specs=[anywhere] * 3,
        out_specs=(anywhere,) * 3,
        scratch_shapes=[sem((3,))],
        compiler_params=pltpu.CompilerParams(vmem_limit_bytes=1 << 20),
    )(blended, gnext, mnext)
    return blended[None], gnext, mnext


def solution(mesh):
    return jax.shard_map(
        functools.partial(body, (4, 4, 4)),
        mesh=mesh,
        in_specs=(
            P(("replica", "fsdp"), None),
            P(("replica", "fsdp"), None),
            P("replica", "fsdp", None),
            P("fsdp", None),
            P(("fsdp", "replica"), None),
            P("replica", "fsdp", None),
        ),
        out_specs=(P("replica", "fsdp", None), P("fsdp", None), P(("fsdp", "replica"), None)),
        check_vma=False,
    )
```
